256 devices in a mesh: ctx: 32 (over z, x_lo, core), tp: 8 (over x_hi, y).
Axes of the slice: x: 4 (x_hi: 2, x_lo: 2; x = x_hi * 2 + x_lo), y: 4, z: 8, core: 2. Of those that a mesh axis runs over, the one named last changes fastest.
Arguments:
- hidden: bfloat16 [32, 128, 8192], P('ctx', None, 'tp'), may hold values from -6 to 6
- norm_gain: bfloat16 [8192], replicated, may hold values from 0.099609375 to 1.8984375
- w_query: bfloat16 [8192, 8192], P('ctx', 'tp'), may hold values from -0.0625 to 0.0625
- key_weight_matrix: bfloat16 [8192, 1024], P('ctx', 'tp'), may hold values from -0.0625 to 0.0625
- value_weight_matrix: bfloat16 [8192, 1024], P('ctx', 'tp'), may hold values from -0.0625 to 0.0625
- key_cache: bfloat16 [32, 512, 1024], P('ctx', None, 'tp'), may hold values from -400 to 400
- stored_value_cache: bfloat16 [32, 512, 1024], P('ctx', None, 'tp'), may hold values from -6 to 6
- sel_rows: int32 [32, 128], P('ctx'), may hold values from 0 to 511, as said below
- span_place: int32 [32], P('ctx'), may hold values from 0 to 31, each once
Outputs:
- attended: bfloat16 [32, 128, 8192], P('ctx', None, 'tp')
- mixed_key_cache: bfloat16 [32, 512, 1024], P('ctx', None, 'tp')
- mixed_value_cache: bfloat16 [32, 512, 1024], P('ctx', None, 'tp')
The draws below stay inside these ranges and needn't reach their ends.
Inputs may be any that keep to these rules, and one draw needn't show every extreme that they name: `sel_rows`: each row lists 128 distinct rows of its span in increasing order; the first and the last row of every span are always listed. `span_place`: every place occurs once.
All inputs are finite; a program needn't handle non-finite values.
Results may differ from the reference program's by a relative error of at most 0.034.
The reference program's roundings to bfloat16 on the way count: a program that leaves them out, or rounds other values in their place, can miss the bound.
Values may be sent and summed in bfloat16 or wider, within the bound.
No kernel may reach another device: no remote copies, remote signals or barrier semaphores. Data moves between devices by JAX's collectives and lax.ppermute only.
A program may use at most 128 MiB of HBM per device.

```python
import jax
import jax.numpy as jnp
from jax import lax

MODEL_WIDTH = 8192
QUERY_HEADS = 64
KEY_VALUE_HEADS = 8
HEAD_WIDTH = 128
SPAN_TOKENS = 512
REDONE_ROWS = 128
SPAN_TOTAL = 32


def draw_key_cache(key, part):
    key = jax.random.fold_in(key, 11)
    first_key = jax.random.fold_in(key, 0)
    array_shape = (SPAN_TOTAL, SPAN_TOKENS, KEY_VALUE_HEADS * HEAD_WIDTH)
    base = jax.random.normal(first_key, array_shape, jnp.float32)
    return jnp.clip(base, -6.0, 6.0).astype(jnp.bfloat16)


def draw_sel_rows(key, part):
    key = jax.random.fold_in(key, 7)
    span_keys = jax.random.split(key, SPAN_TOTAL)

    def pick_rows(span_key):
        shuffled = jax.random.permutation(span_key, SPAN_TOKENS - 2) + 1
        inner = shuffled[:REDONE_ROWS - 2].astype(jnp.int32)
        edges = jnp.array([0, SPAN_TOKENS - 1], dtype=jnp.int32)
        return jnp.sort(jnp.concatenate([edges, inner]))
    return jax.vmap(pick_rows)(span_keys).astype(jnp.int32)


def steps_of(rng, extent, pieces, least, high):
    def one(axis_at, shards_of):
        steps = jax.random.uniform(jax.random.fold_in(jax.random.fold_in(rng, 6), axis_at), (shards_of,), jnp.float32, least / len(pieces), high / len(pieces))
        return jnp.repeat(jnp.exp(steps), extent[axis_at] // shards_of).reshape((-1,) + (1,) * (len(extent) - axis_at - 1))

    factor_of = one(*pieces[0])
    for cut in pieces[1:]:
        factor_of = factor_of * one(*cut)
    return factor_of


def bell_draw(key, dims, spread, bound, cuts=(), kind=jnp.bfloat16):
    values = jax.random.normal(key, dims, jnp.float32) * spread
    if len(cuts) > 0:
        values = steps_of(key, dims, cuts, -0.22, 0.18) * values
    return jnp.clip(values, min=-bound, max=bound).astype(kind)


def setup_inputs(seed: int = 0) -> dict:
    key_list = jax.random.split(jax.random.key(seed), 10)
    return {
        "hidden": bell_draw(key_list[0], (SPAN_TOTAL, REDONE_ROWS, MODEL_WIDTH), 1.0, 6.0, ((0, 32), (2, 8))),
        "norm_gain": jnp.clip(1.0 + 0.18 * jax.random.normal(key_list[1], (MODEL_WIDTH,), jnp.float32), 0.099609375, 1.8984375).astype(jnp.bfloat16),
        "w_query": bell_draw(key_list[2], (MODEL_WIDTH, QUERY_HEADS * HEAD_WIDTH), MODEL_WIDTH ** -0.5, 0.0625, ((0, 32), (1, 8))),
        "key_weight_matrix": bell_draw(key_list[3], (MODEL_WIDTH, KEY_VALUE_HEADS * HEAD_WIDTH), MODEL_WIDTH ** -0.5, 0.0625, ((0, 32), (1, 8))),
        "value_weight_matrix": bell_draw(key_list[4], (MODEL_WIDTH, KEY_VALUE_HEADS * HEAD_WIDTH), MODEL_WIDTH ** -0.5, 0.0625, ((0, 32), (1, 8))),
        "key_cache": draw_key_cache(jax.random.fold_in(key_list[9], 71), 0),
        "stored_value_cache": bell_draw(key_list[6], (SPAN_TOTAL, SPAN_TOKENS, KEY_VALUE_HEADS * HEAD_WIDTH), 1.0, 6.0, ((0, 32), (2, 8))),
        "sel_rows": draw_sel_rows(jax.random.fold_in(key_list[9], 71), 0),
        "span_place": jax.random.permutation(key_list[8], SPAN_TOTAL).astype(jnp.int32),
    }


negative = -1e+30

def normalize(hidden, norm_gain):
    values = hidden.astype(jnp.float32)
    meansq = lax.optimization_barrier(jnp.mean(values * values, axis=-1, keepdims=True))
    return (values * lax.rsqrt(meansq + 1e-05) * norm_gain.astype(jnp.float32)).astype(jnp.bfloat16)

def apply_rotation(vectors, token_positions):
    half_size = vectors.shape[-1] // 2
    freqs = 500000.0 ** (-2.0 * jnp.arange(half_size, dtype=jnp.float32) / vectors.shape[-1])
    angles = token_positions.astype(jnp.float32)[:, None] * freqs[None, :]
    cosine = jnp.cos(angles)[:, None, :]
    sine = jnp.sin(angles)[:, None, :]
    first_half = vectors[..., :half_size]
    second_half = vectors[..., half_size:]
    return jnp.concatenate([first_half * cosine - second_half * sine, second_half * cosine + first_half * sine], axis=-1)

def reference(hidden, norm_gain, w_query, key_weight_matrix, value_weight_matrix, key_cache, stored_value_cache, sel_rows, span_place):
    normed = normalize(hidden, norm_gain).reshape(SPAN_TOTAL * REDONE_ROWS, MODEL_WIDTH)
    proj_query = jnp.dot(normed, w_query, preferred_element_type=jnp.float32)
    projected_key = jnp.dot(normed, key_weight_matrix, preferred_element_type=jnp.float32)
    projected_value = jnp.dot(normed, value_weight_matrix, preferred_element_type=jnp.float32)
    token_positions = (span_place[:, None] * SPAN_TOKENS + sel_rows).reshape(-1).astype(jnp.int32)
    fresh_query = apply_rotation(proj_query.reshape(-1, QUERY_HEADS, HEAD_WIDTH), token_positions).astype(jnp.bfloat16)
    fresh_key = apply_rotation(projected_key.reshape(-1, KEY_VALUE_HEADS, HEAD_WIDTH), token_positions).astype(jnp.bfloat16).reshape(SPAN_TOTAL, REDONE_ROWS, KEY_VALUE_HEADS * HEAD_WIDTH)
    fresh_value = projected_value.astype(jnp.bfloat16).reshape(SPAN_TOTAL, REDONE_ROWS, KEY_VALUE_HEADS * HEAD_WIDTH)
    span_ids = jnp.arange(SPAN_TOTAL, dtype=jnp.int32)[:, None]
    mixed_key_cache = key_cache.at[span_ids, sel_rows].set(fresh_key)
    mixed_value_cache = stored_value_cache.at[span_ids, sel_rows].set(fresh_value)
    every_key_row = mixed_key_cache.reshape(SPAN_TOTAL * SPAN_TOKENS, KEY_VALUE_HEADS, HEAD_WIDTH)
    every_value_row = mixed_value_cache.reshape(SPAN_TOTAL * SPAN_TOKENS, KEY_VALUE_HEADS, HEAD_WIDTH)
    key_positions = (span_place[:, None] * SPAN_TOKENS + jnp.arange(SPAN_TOKENS, dtype=jnp.int32)[None, :]).reshape(-1)
    query_group_width = QUERY_HEADS // KEY_VALUE_HEADS
    scale = HEAD_WIDTH ** (-0.5)
    query_matrix = fresh_query.reshape(SPAN_TOTAL, REDONE_ROWS, KEY_VALUE_HEADS, query_group_width, HEAD_WIDTH)
    query_positions = token_positions.reshape(SPAN_TOTAL, REDONE_ROWS)

    def attend(inputs):
        span_queries, span_positions = inputs
        results = []
        for current_head_index in range(KEY_VALUE_HEADS):
            scores = jnp.einsum('sgd,kd->gsk', span_queries[:, current_head_index].astype(jnp.float32), every_key_row[:, current_head_index].astype(jnp.float32)) * scale
            allowed = key_positions[None, None, :] <= span_positions[None, :, None]
            scores = jnp.where(allowed, scores, negative)
            largest = lax.optimization_barrier(jnp.max(scores, axis=-1, keepdims=True))
            weights = jnp.where(allowed, jnp.exp(scores - largest), 0.0).astype(jnp.bfloat16)
            totals = lax.optimization_barrier(jnp.sum(weights.astype(jnp.float32), axis=-1))
            summed = jnp.einsum('gsk,kd->gsd', weights.astype(jnp.float32), every_value_row[:, current_head_index].astype(jnp.float32))
            results.append(jnp.transpose(summed / totals[..., None], (1, 0, 2)))
        return jnp.stack(results, axis=1).reshape(REDONE_ROWS, QUERY_HEADS * HEAD_WIDTH).astype(jnp.bfloat16)
    attended = lax.map(attend, (query_matrix, query_positions))
    return (attended, mixed_key_cache, mixed_value_cache)
```

```python
import functools
import math

import jax
import jax.numpy as jnp
from jax import lax
from jax.experimental import pallas as pl
from jax.experimental.pallas import tpu as pltpu
from jax.sharding import PartitionSpec as P

HEAD_WIDTH = 128
ROWS = 128
SPAN = 512
WIDTH = 8192
Z = 8
GROUP = 4
CTX = 32
TP = 8
CHUNK = 1024
NEGATIVE = -1e30
SCALE2 = HEAD_WIDTH ** (-0.5) * math.log2(math.e)


def to_group(x, d):
    return lax.ppermute(x, "ctx", [(c, (c // GROUP) * GROUP + ((c % GROUP) ^ d)) for c in range(CTX)])


def along_z(x, s):
    return lax.ppermute(x, "ctx", [(c, (c + GROUP * s) % CTX) for c in range(CTX)])


def along_y(x, s):
    return lax.ppermute(x, "tp", [(t, (t // 4) * 4 + (t + s) % 4) for t in range(TP)])


def along_xh(x):
    return lax.ppermute(x, "tp", [(t, t ^ 4) for t in range(TP)])


def xor_order(x, core, xlo, axis=0):
    a, b, c, d = jnp.split(x, 4, axis=axis)
    swapped = jnp.concatenate([b, a, d, c], axis=axis)
    x = jnp.where(core == 1, swapped, x)
    a, b, c, d = jnp.split(x, 4, axis=axis)
    swapped = jnp.concatenate([c, d, a, b], axis=axis)
    return jnp.where(xlo == 1, swapped, x)


def project_kernel(*refs):
    ids = refs[0]
    gain, cos_q, sin_q, cos_kv, sin_kv = refs[1:6]
    own = refs[6:14]
    other = refs[14:22]
    weights = refs[22:31]
    q_out, kv_out = refs[31:33]
    normed, acc_q, acc_kv = refs[33:36]

    def rows_step(k, carry):
        rows = pl.ds(pl.multiple_of(k * 16, 16), 16)
        for dc, arrays in enumerate((own, other)):
            for dx in range(2):
                total = jnp.zeros((16, 128), jnp.float32)
                for ref in arrays:
                    v = ref[dx, rows, :].astype(jnp.float32)
                    v = v * v
                    for lane in range(0, CHUNK, 128):
                        total = total + v[:, lane : lane + 128]
                inv = lax.rsqrt(jnp.sum(total, axis=1, keepdims=True) / WIDTH + 1e-05)
                for i, ref in enumerate(arrays):
                    place = ids[i]
                    v = ref[dx, rows, :].astype(jnp.float32)
                    v = (v * inv * gain[place]).astype(jnp.bfloat16)
                    normed[place, pl.ds(pl.multiple_of((dc + 2 * dx) * ROWS + k * 16, 16), 16), :] = v
        return carry

    lax.fori_loop(0, ROWS // 16, rows_step, 0)

    row_block = lax.broadcasted_iota(jnp.int32, (256, 256), 0) // 64
    col_block = lax.broadcasted_iota(jnp.int32, (256, 256), 1) // 64
    same = row_block == col_block

    def spread(packed):
        tiled = jnp.concatenate([packed] * 4, axis=0)
        return jnp.where(same, tiled, jnp.zeros_like(tiled))

    for s, ref in enumerate(weights):
        shards = ref.shape[0]
        at = ids[8 + min(s, 7)]
        first = 2 * 256 if s == 8 else 0
        x = normed[at, :, first : first + shards * 256]
        wq = jnp.concatenate([ref[j, :256, :] for j in range(shards)], axis=0)
        wkv = jnp.concatenate([spread(ref[j, 256:320, :]) for j in range(shards)], axis=0)
        pq = jnp.dot(x, wq, preferred_element_type=jnp.float32)
        pkv = jnp.dot(x, wkv, preferred_element_type=jnp.float32)
        if s == 0:
            acc_q[...] = pq
            acc_kv[...] = pkv
        else:
            acc_q[...] += pq
            acc_kv[...] += pkv

    for r in range(4):
        rows = slice(r * ROWS, (r + 1) * ROWS)
        for h in range(2):
            v = acc_q[rows, h * 128 : (h + 1) * 128]
            v = v * cos_q[rows, :] + pltpu.roll(v, 64, axis=1) * sin_q[rows, :]
            q_out[r, :, h * 128 : (h + 1) * 128] = v.T.astype(jnp.bfloat16)
        v = acc_kv[rows, :128] + acc_kv[rows, 128:]
        v = v + pltpu.roll(v, 64, axis=1)
        v = v * cos_kv[rows, :] + pltpu.roll(v, 32, axis=1) * sin_kv[rows, :]
        kv_out[r] = v.astype(jnp.bfloat16)


def vmem_specs(n):
    return [pl.BlockSpec(memory_space=pltpu.VMEM)] * n


def project(ids, gain, tables, own, other, weights):
    return pl.pallas_call(
        project_kernel,
        out_shape=(
            jax.ShapeDtypeStruct((4, 128, 256), jnp.bfloat16),
            jax.ShapeDtypeStruct((4, ROWS, 128), jnp.bfloat16),
        ),
        in_specs=[pl.BlockSpec(memory_space=pltpu.SMEM)] + vmem_specs(30),
        out_specs=tuple(vmem_specs(2)),
        scratch_shapes=[
            pltpu.VMEM((8, 512, CHUNK), jnp.bfloat16),
            pltpu.VMEM((512, 256), jnp.float32),
            pltpu.VMEM((512, 256), jnp.float32),
        ],
        compiler_params=pltpu.CompilerParams(vmem_limit_bytes=44 * 2**20),
        cost_estimate=pl.CostEstimate(flops=2 * 512 * 8192 * 512, bytes_accessed=14 * 2**20, transcendentals=0),
    )(ids, gain, *tables, *own, *other, *weights)


def attend_kernel(block_count, first, last, *refs):
    places = refs[0]
    q, limit = refs[1:3]
    at = 3
    if not first:
        m_in, l_in, acc_in = refs[3:6]
        at = 6
    blocks = refs[at : at + block_count]
    at += block_count
    if last:
        out = refs[at]
        m_ref, l_ref, acc_ref = refs[at + 1 : at + 4]
    else:
        m_ref, l_ref, acc_ref = refs[at : at + 3]

    if first:
        m_ref[...] = jnp.full_like(m_ref, NEGATIVE)
        l_ref[...] = jnp.zeros_like(l_ref)
        acc_ref[...] = jnp.zeros_like(acc_ref)
    else:
        m_ref[...] = m_in[...]
        l_ref[...] = l_in[...]
        acc_ref[...] = acc_in[...]

    def update(ref, dx, r, masked):
        query = q[r]
        halves = [
            jnp.dot(ref[dx, 0:256, h * 128 : (h + 1) * 128], query, preferred_element_type=jnp.float32)
            for h in range(2)
        ]
        if masked:
            for h in range(2):
                row = lax.broadcasted_iota(jnp.int32, (256, 256), 0) + h * 256
                halves[h] = jnp.where(row <= limit[r, 0:1, :], halves[h], NEGATIVE)
        old = m_ref[r, 0:1, :]
        new = jnp.maximum(
            old,
            jnp.maximum(
                jnp.max(halves[0], axis=0, keepdims=True), jnp.max(halves[1], axis=0, keepdims=True)
            ),
        )
        alpha = jnp.exp2((old - new) * SCALE2)
        total = l_ref[r, 0:1, :] * alpha
        acc = acc_ref[r] * alpha
        for h in range(2):
            p = jnp.exp2((halves[h] - new) * SCALE2).astype(jnp.bfloat16)
            total = total + jnp.sum(p.astype(jnp.float32), axis=0, keepdims=True)
            acc = acc + jnp.dot(
                ref[dx, 256 + h * 128 : 384 + h * 128, :], p, preferred_element_type=jnp.float32
            )
        m_ref[r] = jnp.broadcast_to(new, (8, 256))
        l_ref[r] = jnp.broadcast_to(total, (8, 256))
        acc_ref[r] = acc

    for i, ref in enumerate(blocks):

        def step(n, carry, i=i, ref=ref):
            dx = n // 4
            r = n % 4
            key_place = places[4 + 2 * i + dx]
            query_place = places[r]

            @pl.when(key_place < query_place)
            def _():
                update(ref, dx, r, False)

            @pl.when(key_place == query_place)
            def _():
                update(ref, dx, r, True)

            return carry

        lax.fori_loop(0, 4 * ref.shape[0], step, 0)

    if last:
        for r in range(4):
            v = acc_ref[r] / l_ref[r, 0:1, :]
            for h in range(2):
                out[r, :, h * 128 : (h + 1) * 128] = v[:, h * 128 : (h + 1) * 128].T.astype(jnp.bfloat16)


def attend(places, q, limit, state, blocks, last):
    first = state is None
    state_in = [] if first else list(state)
    state_shapes = (
        jax.ShapeDtypeStruct((4, 8, 256), jnp.float32),
        jax.ShapeDtypeStruct((4, 8, 256), jnp.float32),
        jax.ShapeDtypeStruct((4, 128, 256), jnp.float32),
    )
    spans = sum(b.shape[0] for b in blocks)
    if last:
        out_shape = jax.ShapeDtypeStruct((4, ROWS, 256), jnp.bfloat16)
        out_specs = pl.BlockSpec(memory_space=pltpu.VMEM)
        scratch = [pltpu.VMEM(s.shape, s.dtype) for s in state_shapes]
    else:
        out_shape = state_shapes
        out_specs = tuple(vmem_specs(3))
        scratch = []
    return pl.pallas_call(
        functools.partial(attend_kernel, len(blocks), first, last),
        out_shape=out_shape,
        in_specs=[pl.BlockSpec(memory_space=pltpu.SMEM)] + vmem_specs(2 + len(state_in) + len(blocks)),
        out_specs=out_specs,
        scratch_shapes=scratch,
        compiler_params=pltpu.CompilerParams(vmem_limit_bytes=24 * 2**20),
        cost_estimate=pl.CostEstimate(
            flops=spans * 4 * 2 * 2 * 256 * 512 * 256,
            bytes_accessed=spans * 2**18 + 2**20,
            transcendentals=spans * 4 * 512 * 256,
        ),
    )(places, q, limit, *state_in, *blocks)


def on_device(
    hidden,
    norm_gain,
    w_query,
    key_weight_matrix,
    value_weight_matrix,
    key_cache,
    stored_value_cache,
    sel_rows,
    span_place,
):
    c = lax.axis_index("ctx")
    t = lax.axis_index("tp")
    z = c // GROUP
    g = c % GROUP
    core = g % 2
    xlo = g // 2
    xhi = t // 4
    y = t % 4

    info = jnp.concatenate(
        [sel_rows, jnp.broadcast_to(span_place[:, None], (7, ROWS))], axis=0
    )
    info = lax.all_gather(info, "ctx", axis=0, tiled=False)

    def half(w, h):
        return jnp.concatenate([w[:, 32 * h : 32 * h + 32], w[:, 64 + 32 * h : 96 + 32 * h]], axis=1)

    def pack(w):
        return w.reshape(4, 64, 64).transpose(1, 0, 2).reshape(64, 256)

    pieces = jnp.stack(
        [
            jnp.concatenate(
                [
                    w_query[:, 256 * j : 256 * (j + 1)],
                    pack(half(value_weight_matrix if j % 2 else key_weight_matrix, j // 2)),
                ],
                axis=0,
            )
            for j in range(4)
        ]
    )
    shards = [lax.dynamic_index_in_dim(pieces, g, 0, keepdims=True)]
    for d in (1, 2, 3):
        shards.append(to_group(lax.dynamic_index_in_dim(pieces, g ^ d, 0, keepdims=True), d))
    block = xor_order(jnp.concatenate(shards, axis=0), core, xlo)

    x0 = hidden
    pair = jnp.concatenate([x0, to_group(x0, 2)], axis=0)
    far = along_xh(pair)
    pair_r, pair_l = along_y(pair, 1), along_y(pair, -1)
    far_r, far_l = along_y(far, 1), along_y(far, -1)
    pair_2, far_2 = along_y(pair_r, 1), along_y(far_l, -1)
    own = [pair, far, pair_r, pair_l, far_r, far_l, pair_2, far_2]
    own_ids = [
        t,
        t ^ 4,
        xhi * 4 + (y + 3) % 4,
        xhi * 4 + (y + 1) % 4,
        (1 - xhi) * 4 + (y + 3) % 4,
        (1 - xhi) * 4 + (y + 1) % 4,
        xhi * 4 + (y + 2) % 4,
        (1 - xhi) * 4 + (y + 2) % 4,
    ]
    other = [to_group(v, 1) for v in own]

    r1, l1 = along_z(block, 1), along_z(block, -1)
    r2, l2 = along_z(r1, 1), along_z(l1, -1)
    r3, l3 = along_z(r2, 1), along_z(l2, -1)
    r4, l4 = along_z(r3[:2], 1), along_z(l3[2:], -1)
    weights = [block, r1, l1, r2, l2, r3, l3, r4, l4]
    weight_ids = [(z + s) % 8 for s in (0, 7, 1, 6, 2, 5, 3, 4)]
    ids = jnp.stack(own_ids + weight_ids).astype(jnp.int32)

    place_all = info[:, 1, 0].reshape(Z, GROUP)
    place_rel = lax.dynamic_slice_in_dim(jnp.concatenate([place_all, place_all], axis=0), z, Z, 0)
    place_rel = xor_order(place_rel, core, xlo, axis=1)
    sel_rel = lax.dynamic_slice_in_dim(info[:, 0, :], z * GROUP, GROUP, 0)
    sel_rel = xor_order(sel_rel, core, xlo)
    positions = (place_rel[0][:, None] * SPAN + sel_rel).reshape(GROUP * ROWS)
    half_size = HEAD_WIDTH // 2
    freqs = 500000.0 ** (-2.0 * jnp.arange(half_size, dtype=jnp.float32) / HEAD_WIDTH)
    angles = positions.astype(jnp.float32)[:, None] * freqs[None, :]
    cos, sin = jnp.cos(angles), jnp.sin(angles)
    cos_half = jnp.where(xlo == 0, cos[:, :32], cos[:, 32:])
    sin_half = jnp.where(xlo == 0, sin[:, :32], sin[:, 32:])
    cos_half = jnp.where(core == 0, cos_half, 1.0)
    sin_half = jnp.where(core == 0, sin_half, 0.0)
    tables = (
        jnp.concatenate([cos, cos], axis=1),
        jnp.concatenate([-sin, sin], axis=1),
        jnp.concatenate([cos_half] * 4, axis=1),
        jnp.concatenate([-sin_half, sin_half] * 2, axis=1),
    )
    gain = norm_gain.astype(jnp.float32).reshape(8, 1, CHUNK)

    q, kv_piece = project(ids, gain, tables, own, other, weights)

    got = [kv_piece[0]] + [to_group(kv_piece[d], d) for d in (1, 2, 3)]

    def join(a, b):
        low = jnp.where(xlo == 0, a, b)
        high = jnp.where(xlo == 0, b, a)
        return jnp.concatenate([low[:, :32], high[:, :32], low[:, 32:64], high[:, 32:64]], axis=1)

    new_key = join(jnp.where(core == 0, got[0], got[1]), jnp.where(core == 0, got[2], got[3]))
    new_value = join(jnp.where(core == 0, got[1], got[0]), jnp.where(core == 0, got[3], got[2]))
    hints = dict(indices_are_sorted=True, unique_indices=True)
    mixed_key_cache = key_cache[0].at[sel_rows[0]].set(new_key, **hints)
    mixed_value_cache = stored_value_cache[0].at[sel_rows[0]].set(new_value, **hints)

    turned = mixed_value_cache.T
    span_block = jnp.concatenate(
        [
            jnp.concatenate([mixed_key_cache[:256], mixed_key_cache[256:]], axis=1),
            turned[:, :256],
            turned[:, 256:],
        ],
        axis=0,
    )[None]
    a0 = jnp.concatenate([span_block, to_group(span_block, 2)], axis=0)
    ar1, al1 = along_z(a0, 1), along_z(a0, -1)
    ar2, al2 = along_z(ar1, 1), along_z(al1, -1)
    ar3, al3 = along_z(ar2, 1), along_z(al2, -1)
    ar4, al4 = along_z(ar3[:1], 1), along_z(al3[1:], -1)

    limit = jnp.broadcast_to(
        jnp.concatenate([sel_rel, sel_rel], axis=1)[:, None, :], (GROUP, 8, 256)
    )
    state = None
    steps = [([a0], [0]), ([ar1, al1], [7, 1]), ([ar2, al2], [6, 2]), ([ar3, al3], [5, 3]), ([ar4, al4], [4, 4])]
    for n, (arrays, at) in enumerate(steps):
        blocks = []
        places = [place_rel[0]]
        for k, (a, s) in enumerate(zip(arrays, at)):
            blocks += [a, to_group(a, 1)]
            if n == 4:
                places += [place_rel[s, 2 * k], jnp.zeros_like(place_rel[0, 0]), place_rel[s, 2 * k + 1], jnp.zeros_like(place_rel[0, 0])]
            else:
                places += [place_rel[s, 0], place_rel[s, 2], place_rel[s, 1], place_rel[s, 3]]
        places = jnp.concatenate([jnp.atleast_1d(p) for p in places])
        state = attend(places, q, limit, state, blocks, n == 4)

    out = [state[0]] + [to_group(state[d], d) for d in (1, 2, 3)]
    attended = xor_order(jnp.concatenate(out, axis=1), core, xlo, axis=1)
    return (attended[None], mixed_key_cache[None], mixed_value_cache[None])


def solution(mesh):
    return jax.shard_map(
        on_device,
        mesh=mesh,
        in_specs=(
            P("ctx", None, "tp"),
            P(),
            P("ctx", "tp"),
            P("ctx", "tp"),
            P("ctx", "tp"),
            P("ctx", None, "tp"),
            P("ctx", None, "tp"),
            P("ctx", None),
            P("ctx"),
        ),
        out_specs=(P("ctx", None, "tp"), P("ctx", None, "tp"), P("ctx", None, "tp")),
        check_vma=False,
    )
```

```python
import functools
import math

import jax
import jax.numpy as jnp
from jax import lax
from jax.experimental import pallas as pl
from jax.experimental.pallas import tpu as pltpu
from jax.sharding import PartitionSpec as P

HEAD_WIDTH = 128
ROWS = 128
SPAN = 512
WIDTH = 8192
Z = 8
GROUP = 4
CTX = 32
TP = 8
CHUNK = 1024
NEGATIVE = -1e30
BLOCK_ROWS = 528
SCALE2 = HEAD_WIDTH ** (-0.5) * math.log2(math.e)


def to_group(x, d):
    return lax.ppermute(x, "ctx", [(c, (c // GROUP) * GROUP + ((c % GROUP) ^ d)) for c in range(CTX)])


def along_z(x):
    return lax.ppermute(x, "ctx", [(c, (c + (GROUP if c % 2 == 0 else -GROUP)) % CTX) for c in range(CTX)])


def shift_z(x, s):
    return lax.ppermute(x, "ctx", [(c, (c + GROUP * s) % CTX) for c in range(CTX)])


def along_y(x):
    def place(c, t, s):
        return c * TP + (t // 4) * 4 + (t + s) % 4

    return lax.ppermute(
        x,
        ("ctx", "tp"),
        [(place(c, t, 0), place(c, t, 1 if c % 2 == 0 else -1)) for c in range(CTX) for t in range(TP)],
    )


def along_xh(x):
    return lax.ppermute(x, "tp", [(t, t ^ 4) for t in range(TP)])


def xor_order(x, core, xlo, axis=0):
    a, b, c, d = jnp.split(x, 4, axis=axis)
    swapped = jnp.concatenate([b, a, d, c], axis=axis)
    x = jnp.where(core == 1, swapped, x)
    a, b, c, d = jnp.split(x, 4, axis=axis)
    swapped = jnp.concatenate([c, d, a, b], axis=axis)
    return jnp.where(xlo == 1, swapped, x)


def vmem_specs(n):
    return [pl.BlockSpec(memory_space=pltpu.VMEM)] * n


SMEM_SPEC = pl.BlockSpec(memory_space=pltpu.SMEM)


def normalize_kernel(*refs):
    ids, gain = refs[:2]
    arrays = refs[2:10]
    normed = refs[10]

    def rows_step(k, carry):
        rows = pl.ds(pl.multiple_of(k * 16, 16), 16)
        for j in range(4):
            to = ids[8 + j] * ROWS + k * 16
            total = jnp.zeros((16, 128), jnp.float32)
            for ref in arrays:
                v = ref[j, rows, :].astype(jnp.float32)
                v = v * v
                for lane in range(0, CHUNK, 128):
                    total = total + v[:, lane : lane + 128]
            inv = lax.rsqrt(jnp.sum(total, axis=1, keepdims=True) / WIDTH + 1e-05)
            for i, ref in enumerate(arrays):
                place = ids[i]
                v = ref[j, rows, :].astype(jnp.float32)
                v = (v * inv * gain[place]).astype(jnp.bfloat16)
                normed[place, pl.ds(pl.multiple_of(to, 16), 16), :] = v
        return carry

    lax.fori_loop(0, ROWS // 16, rows_step, 0)


def normalize(ids, gain, arrays):
    return pl.pallas_call(
        normalize_kernel,
        out_shape=jax.ShapeDtypeStruct((8, 512, CHUNK), jnp.bfloat16),
        in_specs=[SMEM_SPEC] + vmem_specs(9),
        out_specs=vmem_specs(1)[0],
        compiler_params=pltpu.CompilerParams(vmem_limit_bytes=24 * 2**20),
        cost_estimate=pl.CostEstimate(flops=6 * 10**9, bytes_accessed=16 * 2**20, transcendentals=0),
    )(ids, gain, *arrays)


def product(x, ref):
    row_block = lax.broadcasted_iota(jnp.int32, (256, 256), 0) // 64
    col_block = lax.broadcasted_iota(jnp.int32, (256, 256), 1) // 64
    same = row_block == col_block

    def spread(packed):
        tiled = jnp.concatenate([packed] * 4, axis=0)
        return jnp.where(same, tiled, jnp.zeros_like(tiled))

    shards = ref.shape[0]
    wq = jnp.concatenate([ref[j, :256, :] for j in range(shards)], axis=0)
    wkv = jnp.concatenate([spread(ref[j, 256:320, :]) for j in range(shards)], axis=0)
    pq = jnp.dot(x, wq, preferred_element_type=jnp.float32)
    pkv = jnp.dot(x, wkv, preferred_element_type=jnp.float32)
    return pq, pkv


def multiply_kernel(ids, normed, *refs):
    weights, (acc_q, acc_kv) = refs[:-2], refs[-2:]
    for s, ref in enumerate(weights):
        pq, pkv = product(normed[ids[s]], ref)
        if s == 0:
            acc_q[...] = pq
            acc_kv[...] = pkv
        else:
            acc_q[...] += pq
            acc_kv[...] += pkv


def multiply(ids, normed, weights):
    return pl.pallas_call(
        multiply_kernel,
        out_shape=(jax.ShapeDtypeStruct((512, 256), jnp.float32),) * 2,
        in_specs=[SMEM_SPEC] + vmem_specs(1 + len(weights)),
        out_specs=tuple(vmem_specs(2)),
        compiler_params=pltpu.CompilerParams(vmem_limit_bytes=30 * 2**20),
        cost_estimate=pl.CostEstimate(flops=5 * 10**9, bytes_accessed=12 * 2**20, transcendentals=0),
    )(ids, normed, *weights)


def finish_kernel(ids, normed, acc_q_in, acc_kv_in, low, high, cos_q, sin_q, cos_kv, sin_kv, q_out, kv_out, acc_q, acc_kv):
    at = ids[0]
    for n, ref in enumerate((low, high)):
        x = normed[at, :, 512 * n : 512 * (n + 1)]
        pq, pkv = product(x, ref)
        if n == 0:
            acc_q[...] = acc_q_in[...] + pq
            acc_kv[...] = acc_kv_in[...] + pkv
        else:
            acc_q[...] += pq
            acc_kv[...] += pkv
    for r in range(4):
        rows = slice(r * ROWS, (r + 1) * ROWS)
        for h in range(2):
            v = acc_q[rows, h * 128 : (h + 1) * 128]
            v = v * cos_q[rows, :] + pltpu.roll(v, 64, axis=1) * sin_q[rows, :]
            q_out[r, :, h * 128 : (h + 1) * 128] = v.T.astype(jnp.bfloat16)
    lane = lax.broadcasted_iota(jnp.int32, (ROWS, 128), 1)
    pieces = []
    for r in range(4):
        rows = slice(r * ROWS, (r + 1) * ROWS)
        v = acc_kv[rows, :128] + acc_kv[rows, 128:]
        v = v + pltpu.roll(v, 64, axis=1)
        pieces.append(v * cos_kv[rows, :] + pltpu.roll(v, 32, axis=1) * sin_kv[rows, :])
    for r in range(2):
        kv_out[r] = jnp.where(lane < 64, pieces[r], pieces[r + 2]).astype(jnp.bfloat16)


def finish(ids, normed, acc, low, high, tables):
    return pl.pallas_call(
        finish_kernel,
        out_shape=(
            jax.ShapeDtypeStruct((4, 128, 256), jnp.bfloat16),
            jax.ShapeDtypeStruct((2, ROWS, 128), jnp.bfloat16),
        ),
        in_specs=[SMEM_SPEC] + vmem_specs(9),
        out_specs=tuple(vmem_specs(2)),
        scratch_shapes=[pltpu.VMEM((512, 256), jnp.float32)] * 2,
        compiler_params=pltpu.CompilerParams(vmem_limit_bytes=24 * 2**20),
        cost_estimate=pl.CostEstimate(flops=2 * 512 * CHUNK * 512, bytes_accessed=6 * 2**20, transcendentals=0),
    )(ids, normed, *acc, low, high, *tables)


def blend_kernel(info, sel, g0, g1, g2, g3, c0, c1, c2, c3, key_out, value_out, block):
    core, xlo, g = info[0], info[1], info[2]
    lane = lax.broadcasted_iota(jnp.int32, (ROWS, 128), 1)
    row = lax.broadcasted_iota(jnp.int32, (SPAN, ROWS), 0)
    pieces = []
    for ref in (g0, g1, g2, g3):
        ends = []
        for r in range(2):
            v = ref[r].astype(jnp.float32)
            turned = pltpu.roll(v, 64, axis=1)
            ends.append((jnp.where(lane < 64, v, turned), jnp.where(lane < 64, turned, v)))
        pieces.append([ends[0][0], ends[1][0], ends[0][1], ends[1][1]])

    def join(a, b):
        low = jnp.where(xlo == 0, a, b)
        high = jnp.where(xlo == 0, b, a)
        new = jnp.where(lane < 96, pltpu.roll(low, 32, axis=1), high)
        new = jnp.where(lane < 64, pltpu.roll(high, 32, axis=1), new)
        return jnp.where(lane < 32, low, new).astype(jnp.bfloat16)

    for d, caches in enumerate((c0, c1, c2, c3)):
        j = jnp.bitwise_xor(g, d)
        got = [pieces[e][d ^ e] for e in range(4)]
        new_key = join(jnp.where(core == 0, got[0], got[1]), jnp.where(core == 0, got[2], got[3]))
        new_value = join(jnp.where(core == 0, got[1], got[0]), jnp.where(core == 0, got[3], got[2]))
        hit = (row == sel[d : d + 1, :]).astype(jnp.float32)
        chosen = jnp.sum(hit, axis=1, keepdims=True) > 0.0
        hit = hit.astype(jnp.bfloat16)
        mixed = []
        for k, new in enumerate((new_key, new_value)):
            placed = jnp.dot(hit, new, preferred_element_type=jnp.float32)
            mixed.append(jnp.where(chosen, placed, caches[k].astype(jnp.float32)))
        if d == 0:
            key_out[...] = mixed[0].astype(jnp.bfloat16)
            value_out[...] = mixed[1].astype(jnp.bfloat16)
        block[j, 0:256, 0:128] = mixed[0][:256].astype(jnp.bfloat16)
        block[j, 0:256, 128:256] = mixed[0][256:].astype(jnp.bfloat16)
        for h in range(2):
            block[j, 256 + 128 * h : 384 + 128 * h, :] = mixed[1][256 * h : 256 * (h + 1)].T.astype(jnp.bfloat16)
        place = info[3 + d].astype(jnp.float32)
        block[j, 512:528, :] = jnp.full((16, 256), place, jnp.float32).astype(jnp.bfloat16)


def blend(info, sel, got, caches):
    cache = jax.ShapeDtypeStruct((SPAN, HEAD_WIDTH), jnp.bfloat16)
    return pl.pallas_call(
        blend_kernel,
        out_shape=(cache, cache, jax.ShapeDtypeStruct((4, BLOCK_ROWS, 256), jnp.bfloat16)),
        in_specs=[SMEM_SPEC] + vmem_specs(9),
        out_specs=tuple(vmem_specs(3)),
        compiler_params=pltpu.CompilerParams(vmem_limit_bytes=16 * 2**20),
        cost_estimate=pl.CostEstimate(flops=4 * 10**9, bytes_accessed=2**22, transcendentals=0),
    )(info, sel, *got, *caches)


def attend_kernel(groups, count, first, last, *refs):
    places, q, limit = refs[:3]
    at = 3
    if not first:
        m_in, acc_in = refs[3:5]
        at = 5
    blocks = refs[at : at + count]
    at += count
    if last:
        out, m_ref, acc_ref = refs[at : at + 3]
    else:
        m_ref, acc_ref = refs[at : at + 2]

    if first:
        m_ref[...] = jnp.full_like(m_ref, NEGATIVE)
        acc_ref[...] = jnp.zeros_like(acc_ref)
    else:
        m_ref[...] = m_in[...]
        acc_ref[...] = acc_in[...]
    ones = jnp.ones((16, 256), jnp.bfloat16)

    def update(spans, r, masked):
        query = q[r]
        chunks = []
        for i, dx in spans:
            for h in range(2):
                s = jnp.dot(
                    blocks[i][dx, 0:256, h * 128 : (h + 1) * 128], query, preferred_element_type=jnp.float32
                )
                if masked:
                    row = lax.broadcasted_iota(jnp.int32, (256, 256), 0) + h * 256
                    s = jnp.where(row <= limit[r, 0:1, :], s, NEGATIVE)
                chunks.append((s, i, dx, h))
        old = m_ref[r, 0:1, :]
        new = old
        for s, _, _, _ in chunks:
            new = jnp.maximum(new, jnp.max(s, axis=0, keepdims=True))
        acc = acc_ref[r] * jnp.exp2((old - new) * SCALE2)
        for s, i, dx, h in chunks:
            p = jnp.exp2((s - new) * SCALE2).astype(jnp.bfloat16)
            values = jnp.concatenate([blocks[i][dx, 256 + h * 128 : 384 + h * 128, :], ones], axis=0)
            acc = acc + jnp.dot(values, p, preferred_element_type=jnp.float32)
        m_ref[r] = jnp.broadcast_to(new, (8, 256))
        acc_ref[r] = acc

    key_places = {}
    for spans in groups:
        for i, dx in spans:
            key_places[i, dx] = jnp.max(blocks[i][dx, 512:528, 0:128].astype(jnp.float32)).astype(jnp.int32)

    def step(r, carry):
        query_place = places[r]
        for spans in groups:
            before = [key_places[k] < query_place for k in spans]
            if first:
                singles = before
            else:
                both = before[0] & before[1]
                singles = [b & ~both for b in before]

                @pl.when(both)
                def _(spans=spans):
                    update(spans, r, False)

            for k, single in zip(spans, singles):

                @pl.when(single)
                def _(k=k):
                    update([k], r, False)

                if first:

                    @pl.when(key_places[k] == query_place)
                    def _(k=k):
                        update([k], r, True)

        return carry

    lax.fori_loop(0, GROUP, step, 0)

    if last:
        for r in range(4):
            v = acc_ref[r, 0:128, :] / acc_ref[r, 128:129, :]
            for h in range(2):
                out[r, :, h * 128 : (h + 1) * 128] = v[:, h * 128 : (h + 1) * 128].T.astype(jnp.bfloat16)


def attend(places, q, limit, state, blocks, groups, last):
    first = state is None
    state_in = [] if first else list(state)
    state_shapes = (
        jax.ShapeDtypeStruct((4, 8, 256), jnp.float32),
        jax.ShapeDtypeStruct((4, 144, 256), jnp.float32),
    )
    spans = sum(b.shape[0] for b in blocks)
    if last:
        out_shape = jax.ShapeDtypeStruct((4, ROWS, 256), jnp.bfloat16)
        out_specs = vmem_specs(1)[0]
        scratch = [pltpu.VMEM(s.shape, s.dtype) for s in state_shapes]
    else:
        out_shape = state_shapes
        out_specs = tuple(vmem_specs(2))
        scratch = []
    return pl.pallas_call(
        functools.partial(attend_kernel, groups, len(blocks), first, last),
        out_shape=out_shape,
        in_specs=[SMEM_SPEC] + vmem_specs(2 + len(state_in) + len(blocks)),
        out_specs=out_specs,
        scratch_shapes=scratch,
        compiler_params=pltpu.CompilerParams(vmem_limit_bytes=16 * 2**20),
        cost_estimate=pl.CostEstimate(
            flops=spans * 16 * 10**8,
            bytes_accessed=spans * 2**18 + 2**20,
            transcendentals=spans * 4 * 512 * 256,
        ),
    )(places, q, limit, *state_in, *blocks)


def on_device(
    hidden,
    norm_gain,
    w_query,
    key_weight_matrix,
    value_weight_matrix,
    key_cache,
    stored_value_cache,
    sel_rows,
    span_place,
):
    c = lax.axis_index("ctx")
    t = lax.axis_index("tp")
    z = c // GROUP
    g = c % GROUP
    core = g % 2
    xlo = g // 2
    xhi = t // 4
    y = t % 4

    info = jnp.concatenate([sel_rows, jnp.broadcast_to(span_place[:, None], (1, ROWS))], axis=0)
    info_x = to_group(info, 2)
    info_c = to_group(jnp.stack([info, info_x]), 1)
    info = jnp.stack([info, info_c[0], info_x, info_c[1]])
    sel_rel = info[:, 0, :]
    place_rel = info[:, 1, 0]

    def by_core(mine, theirs, axis):
        return jnp.where(core == 0, jnp.stack([mine, theirs], axis), jnp.stack([theirs, mine], axis))

    def by_xlo(mine, theirs, axis):
        return jnp.where(xlo == 0, jnp.stack([mine, theirs], axis), jnp.stack([theirs, mine], axis))

    def half(w, h):
        return jnp.concatenate([w[:, 32 * h : 32 * h + 32], w[:, 64 + 32 * h : 96 + 32 * h]], axis=1)

    def pack(w):
        return w.reshape(4, 64, 64).transpose(1, 0, 2).reshape(64, 256)

    pieces = jnp.stack(
        [
            jnp.concatenate(
                [
                    w_query[:, 256 * j : 256 * (j + 1)],
                    pack(half(value_weight_matrix if j % 2 else key_weight_matrix, j // 2)),
                ],
                axis=0,
            )
            for j in range(4)
        ]
    )
    hold = lax.optimization_barrier
    hidden_x = to_group(hidden[0], 2)
    pieces, hidden_x = hold((pieces, hidden_x))
    shards = [lax.dynamic_index_in_dim(pieces, g, 0, keepdims=True)]
    for d in (1, 2, 3):
        shards.append(to_group(lax.dynamic_index_in_dim(pieces, g ^ d, 0, keepdims=True), d))
    block = xor_order(jnp.concatenate(shards, axis=0), core, xlo)
    pair = by_xlo(hidden[0], hidden_x, 0)
    rows = by_core(pair, to_group(pair, 1), 1).reshape(4, ROWS, CHUNK)

    r1, l1 = shift_z(block, 1), shift_z(block, -1)
    far = along_xh(pair)
    y1 = along_y(rows)
    r1, l1, far, y1 = hold((r1, l1, far, y1))
    r2, l2 = shift_z(r1, 1), shift_z(l1, -1)
    far = by_core(far, to_group(far, 1), 1).reshape(4, ROWS, CHUNK)
    f1 = along_y(far)
    y1_other = to_group(y1, 1)
    caches = jnp.stack([key_cache[0], stored_value_cache[0]])
    caches_x = to_group(caches, 2)
    r2, l2, f1, caches_x = hold((r2, l2, f1, caches_x))
    r3, l3 = shift_z(r2, 1), shift_z(l2, -1)
    y2 = along_y(jnp.where(core == 0, y1, f1))
    f1_other = to_group(f1, 1)
    caches_c, caches_d = to_group(caches, 1), to_group(caches_x, 1)
    r3, l3, y2, caches_c, caches_d = hold((r3, l3, y2, caches_c, caches_d))
    r4, l4 = shift_z(r3[:2], 1), shift_z(l3[2:], -1)
    y2_other = to_group(y2, 1)
    arrays = [rows, far, y1, y1_other, f1, f1_other, y2, y2_other]
    down = (y + 3 + 2 * core) % 4
    up = (y + 1 + 2 * core) % 4
    across = (y + 2) % 4
    row_ids = [
        t,
        t ^ 4,
        xhi * 4 + down,
        xhi * 4 + up,
        (1 - xhi) * 4 + down,
        (1 - xhi) * 4 + up,
        (xhi ^ core) * 4 + across,
        (xhi ^ (1 - core)) * 4 + across,
    ]
    row_ids = jnp.stack(row_ids + [j ^ g for j in range(4)]).astype(jnp.int32)
    weight_ids = jnp.stack([(z + s) % 8 for s in (0, 7, 1, 6, 2, 5, 3)]).astype(jnp.int32)
    last_ids = ((z + 4) % 8).astype(jnp.int32)[None]

    positions = (place_rel[:, None] * SPAN + sel_rel).reshape(GROUP * ROWS)
    half_size = HEAD_WIDTH // 2
    freqs = 500000.0 ** (-2.0 * jnp.arange(half_size, dtype=jnp.float32) / HEAD_WIDTH)
    angles = positions.astype(jnp.float32)[:, None] * freqs[None, :]
    cos, sin = jnp.cos(angles), jnp.sin(angles)
    cos_half = jnp.where(xlo == 0, cos[:, :32], cos[:, 32:])
    sin_half = jnp.where(xlo == 0, sin[:, :32], sin[:, 32:])
    cos_half = jnp.where(core == 0, cos_half, 1.0)
    sin_half = jnp.where(core == 0, sin_half, 0.0)
    tables = (
        jnp.concatenate([cos, cos], axis=1),
        jnp.concatenate([-sin, sin], axis=1),
        jnp.concatenate([cos_half] * 4, axis=1),
        jnp.concatenate([-sin_half, sin_half] * 2, axis=1),
    )
    gain = norm_gain.astype(jnp.float32).reshape(8, 1, CHUNK)

    normed = normalize(row_ids, gain, arrays)
    acc = multiply(weight_ids, normed, [block, r1, l1, r2, l2, r3, l3])
    r4, l4, acc = hold((r4, l4, acc))
    q, kv_piece = finish(last_ids, normed, acc, r4, l4, tables)

    got = [kv_piece] + [to_group(kv_piece, d) for d in (1, 2, 3)]
    blend_info = jnp.concatenate([jnp.stack([core, xlo, g]).astype(jnp.int32), place_rel])
    mixed_key_cache, mixed_value_cache, a0 = blend(
        blend_info, sel_rel, got, [caches, caches_c, caches_x, caches_d]
    )

    limit = jnp.broadcast_to(
        jnp.concatenate([sel_rel, sel_rel], axis=1)[:, None, :], (GROUP, 8, 256)
    )
    a1 = along_z(a0)
    state = attend(place_rel, q, limit, None, [a0], [((0, 0), (0, 1)), ((0, 2), (0, 3))], False)
    pairs = [((i, k), (i, k + 1)) for i in range(2) for k in (0, 2)]
    a = a1
    for n in (1, 2, 3):
        a, state = hold((a, state))
        ahead = along_z(a if n < 3 else lax.dynamic_slice_in_dim(a, 2 * core, 2, 0))
        state = attend(place_rel, q, limit, state, [a, to_group(a, 1)], pairs, False)
        a = ahead
    a, state = hold((a, state))
    state = attend(place_rel, q, limit, state, [a, to_group(a, 1)], [((0, 0), (0, 1)), ((1, 0), (1, 1))], True)

    out = [state[0]] + [to_group(state[d], d) for d in (1, 2, 3)]
    attended = xor_order(jnp.concatenate(out, axis=1), core, xlo, axis=1)
    return (attended[None], mixed_key_cache[None], mixed_value_cache[None])


def solution(mesh):
    return jax.shard_map(
        on_device,
        mesh=mesh,
        in_specs=(
            P("ctx", None, "tp"),
            P(),
            P("ctx", "tp"),
            P("ctx", "tp"),
            P("ctx", "tp"),
            P("ctx", None, "tp"),
            P("ctx", None, "tp"),
            P("ctx", None),
            P("ctx"),
        ),
        out_specs=(P("ctx", None, "tp"), P("ctx", None, "tp"), P("ctx", None, "tp")),
        check_vma=False,
    )
```

```python
import functools
import math

import jax
import jax.numpy as jnp
from jax import lax
from jax.experimental import pallas as pl
from jax.experimental.pallas import tpu as pltpu
from jax.sharding import PartitionSpec as P

HEAD_WIDTH = 128
ROWS = 128
SPAN = 512
WIDTH = 8192
Z = 8
GROUP = 4
CTX = 32
TP = 8
CHUNK = 1024
NEGATIVE = -1e30
BLOCK_ROWS = 528
SCALE2 = HEAD_WIDTH ** (-0.5) * math.log2(math.e)


def to_group(x, d):
    return lax.ppermute(x, "ctx", [(c, (c // GROUP) * GROUP + ((c % GROUP) ^ d)) for c in range(CTX)])


def shift_z(x, s):
    return lax.ppermute(x, "ctx", [(c, (c + GROUP * s) % CTX) for c in range(CTX)])


def along_y(x):
    def place(c, t, s):
        return c * TP + (t // 4) * 4 + (t + s) % 4

    return lax.ppermute(
        x,
        ("ctx", "tp"),
        [(place(c, t, 0), place(c, t, 1 if c % 2 == 0 else -1)) for c in range(CTX) for t in range(TP)],
    )


def along_xh(x):
    return lax.ppermute(x, "tp", [(t, t ^ 4) for t in range(TP)])


def xor_order(x, core, xlo, axis=0):
    a, b, c, d = jnp.split(x, 4, axis=axis)
    swapped = jnp.concatenate([b, a, d, c], axis=axis)
    x = jnp.where(core == 1, swapped, x)
    a, b, c, d = jnp.split(x, 4, axis=axis)
    swapped = jnp.concatenate([c, d, a, b], axis=axis)
    return jnp.where(xlo == 1, swapped, x)


def vmem_specs(n):
    return [pl.BlockSpec(memory_space=pltpu.VMEM)] * n


SMEM_SPEC = pl.BlockSpec(memory_space=pltpu.SMEM)


def normalize_kernel(*refs):
    ids, gain = refs[:2]
    arrays = refs[2:10]
    normed = refs[10]

    def rows_step(k, carry):
        rows = pl.ds(pl.multiple_of(k * 16, 16), 16)
        for j in range(4):
            to = ids[8 + j] * ROWS + k * 16
            total = jnp.zeros((16, 128), jnp.float32)
            for ref in arrays:
                v = ref[j, rows, :].astype(jnp.float32)
                v = v * v
                for lane in range(0, CHUNK, 128):
                    total = total + v[:, lane : lane + 128]
            inv = lax.rsqrt(jnp.sum(total, axis=1, keepdims=True) / WIDTH + 1e-05)
            for i, ref in enumerate(arrays):
                place = ids[i]
                v = ref[j, rows, :].astype(jnp.float32)
                v = (v * inv * gain[place]).astype(jnp.bfloat16)
                normed[place, pl.ds(pl.multiple_of(to, 16), 16), :] = v
        return carry

    lax.fori_loop(0, ROWS // 16, rows_step, 0)


def normalize(ids, gain, arrays):
    return pl.pallas_call(
        normalize_kernel,
        out_shape=jax.ShapeDtypeStruct((8, 512, CHUNK), jnp.bfloat16),
        in_specs=[SMEM_SPEC] + vmem_specs(9),
        out_specs=vmem_specs(1)[0],
        compiler_params=pltpu.CompilerParams(vmem_limit_bytes=24 * 2**20),
        cost_estimate=pl.CostEstimate(flops=6 * 10**9, bytes_accessed=16 * 2**20, transcendentals=0),
    )(ids, gain, *arrays)


def multiply_add(acc, ids, normed, weights, part):
    for s, ref in enumerate(weights):
        shards = ref.shape[0]
        first = 512 if s == 8 else 0
        x = normed[ids[min(s, 7)], :, first : first + shards * 256]
        w = jnp.concatenate([part(ref, j) for j in range(shards)], axis=0)
        v = jnp.dot(x, w, preferred_element_type=jnp.float32)
        if s == 0:
            acc[...] = v
        else:
            acc[...] += v


def project_kv_kernel(ids, normed, cos_kv, sin_kv, *refs):
    weights, (kv_out, acc) = refs[:-2], refs[-2:]
    row_block = lax.broadcasted_iota(jnp.int32, (256, 256), 0) // 64
    col_block = lax.broadcasted_iota(jnp.int32, (256, 256), 1) // 64
    same = row_block == col_block

    def spread(ref, j):
        tiled = jnp.concatenate([ref[j, ref.shape[1] - 64 :, :]] * 4, axis=0)
        return jnp.where(same, tiled, jnp.zeros_like(tiled))

    multiply_add(acc, ids, normed, weights, spread)
    lane = lax.broadcasted_iota(jnp.int32, (ROWS, 128), 1)
    pieces = []
    for r in range(4):
        rows = slice(r * ROWS, (r + 1) * ROWS)
        v = acc[rows, :128] + acc[rows, 128:]
        v = v + pltpu.roll(v, 64, axis=1)
        pieces.append(v * cos_kv[rows, :] + pltpu.roll(v, 32, axis=1) * sin_kv[rows, :])
    for r in range(2):
        kv_out[r] = jnp.where(lane < 64, pieces[r], pieces[r + 2]).astype(jnp.bfloat16)


def project_q_kernel(ids, normed, cos_q, sin_q, *refs):
    weights, (q_out, acc) = refs[:-2], refs[-2:]
    multiply_add(acc, ids, normed, weights, lambda ref, j: ref[j, :256, :])
    for r in range(4):
        rows = slice(r * ROWS, (r + 1) * ROWS)
        for h in range(2):
            v = acc[rows, h * 128 : (h + 1) * 128]
            v = v * cos_q[rows, :] + pltpu.roll(v, 64, axis=1) * sin_q[rows, :]
            q_out[:, (2 * r + h) * 128 : (2 * r + h + 1) * 128] = v.T.astype(jnp.bfloat16)


def project(kernel, shape, ids, normed, cos, sin, weights):
    return pl.pallas_call(
        kernel,
        out_shape=jax.ShapeDtypeStruct(shape, jnp.bfloat16),
        in_specs=[SMEM_SPEC] + vmem_specs(3 + len(weights)),
        out_specs=vmem_specs(1)[0],
        scratch_shapes=[pltpu.VMEM((512, 256), jnp.float32)],
        compiler_params=pltpu.CompilerParams(vmem_limit_bytes=24 * 2**20),
        cost_estimate=pl.CostEstimate(flops=4 * 10**9, bytes_accessed=12 * 2**20, transcendentals=0),
    )(ids, normed, cos, sin, *weights)


def blend_kernel(info, sel, g0, g1, g2, g3, c0, c1, c2, c3, key_out, value_out, own_block, other_block):
    core, xlo = info[0], info[1]
    lane = lax.broadcasted_iota(jnp.int32, (ROWS, 128), 1)
    row = lax.broadcasted_iota(jnp.int32, (SPAN, ROWS), 0)
    pieces = []
    for ref in (g0, g1, g2, g3):
        ends = []
        for r in range(2):
            v = ref[r].astype(jnp.float32)
            turned = pltpu.roll(v, 64, axis=1)
            ends.append((jnp.where(lane < 64, v, turned), jnp.where(lane < 64, turned, v)))
        pieces.append([ends[0][0], ends[1][0], ends[0][1], ends[1][1]])

    def join(a, b):
        low = jnp.where(xlo == 0, a, b)
        high = jnp.where(xlo == 0, b, a)
        new = jnp.where(lane < 96, pltpu.roll(low, 32, axis=1), high)
        new = jnp.where(lane < 64, pltpu.roll(high, 32, axis=1), new)
        return jnp.where(lane < 32, low, new).astype(jnp.bfloat16)

    for d, caches in enumerate((c0, c1, c2, c3)):
        block, j = (other_block if d % 2 else own_block), d // 2
        got = [pieces[e][d ^ e] for e in range(4)]
        new_key = join(jnp.where(core == 0, got[0], got[1]), jnp.where(core == 0, got[2], got[3]))
        new_value = join(jnp.where(core == 0, got[1], got[0]), jnp.where(core == 0, got[3], got[2]))
        hit = (row == sel[d : d + 1, :]).astype(jnp.float32)
        chosen = jnp.sum(hit, axis=1, keepdims=True) > 0.0
        hit = hit.astype(jnp.bfloat16)
        mixed = []
        for k, new in enumerate((new_key, new_value)):
            placed = jnp.dot(hit, new, preferred_element_type=jnp.float32)
            mixed.append(jnp.where(chosen, placed, caches[k].astype(jnp.float32)))
        if d == 0:
            key_out[...] = mixed[0].astype(jnp.bfloat16)
            value_out[...] = mixed[1].astype(jnp.bfloat16)
        block[j, 0:256, 0:128] = mixed[0][:256].astype(jnp.bfloat16)
        block[j, 0:256, 128:256] = mixed[0][256:].astype(jnp.bfloat16)
        for h in range(2):
            block[j, 256 + 128 * h : 384 + 128 * h, :] = mixed[1][256 * h : 256 * (h + 1)].T.astype(jnp.bfloat16)
        place = info[2 + d].astype(jnp.float32)
        block[j, 512:528, :] = jnp.full((16, 256), place, jnp.float32).astype(jnp.bfloat16)


def blend(info, sel, got, caches):
    cache = jax.ShapeDtypeStruct((SPAN, HEAD_WIDTH), jnp.bfloat16)
    return pl.pallas_call(
        blend_kernel,
        out_shape=(cache, cache) + (jax.ShapeDtypeStruct((2, BLOCK_ROWS, 256), jnp.bfloat16),) * 2,
        in_specs=[SMEM_SPEC] + vmem_specs(9),
        out_specs=tuple(vmem_specs(4)),
        compiler_params=pltpu.CompilerParams(vmem_limit_bytes=16 * 2**20),
        cost_estimate=pl.CostEstimate(flops=4 * 10**9, bytes_accessed=2**22, transcendentals=0),
    )(info, sel, *got, *caches)


def attend_kernel(count, first, last, top, q, query_place, limit, *refs):
    if not first:
        m_in, acc_in = refs[:2]
        refs = refs[2:]
    blocks, refs = refs[:count], refs[count:]
    if last:
        out, m_ref, acc_ref = refs
    else:
        m_ref, acc_ref = refs
    spans = [(ref, k) for ref in blocks for k in range(ref.shape[0])]
    ones = jnp.ones((16, 256), jnp.bfloat16)
    if first:
        m_ref[...] = jnp.full_like(m_ref, NEGATIVE)
        acc_ref[...] = jnp.zeros_like(acc_ref)
    else:
        m_ref[...] = m_in[...]
        acc_ref[...] = acc_in[...]
    places = [jnp.max(ref[k, 512:528, 0:128].astype(jnp.float32)) for ref, k in spans]
    least = functools.reduce(jnp.minimum, places)

    @pl.when(least <= top[0].astype(jnp.float32))
    def _():
        mine = query_place[0:1, :]
        allowed = [(p <= mine) if first else (p < mine) for p in places]
        chunks = []
        for k, (ref, at) in enumerate(spans):
            for h in range(2):
                s = jnp.dot(ref[at, 0:256, h * 128 : (h + 1) * 128], q[...], preferred_element_type=jnp.float32)
                if first:
                    row = lax.broadcasted_iota(jnp.int32, s.shape, 0) + h * 256
                    s = jnp.where(row <= jnp.where(places[k] == mine, limit[0:1, :], SPAN), s, NEGATIVE)
                chunks.append((s, k, h))
        old = m_ref[0:1, :]
        new = old
        for s, k, h in chunks:
            new = jnp.maximum(new, jnp.where(allowed[k], jnp.max(s, axis=0, keepdims=True), NEGATIVE))
        acc = acc_ref[...] * jnp.exp2((old - new) * SCALE2)
        against = [jnp.where(a, new, -NEGATIVE) for a in allowed]
        for s, k, h in chunks:
            p = jnp.exp2((s - against[k]) * SCALE2).astype(jnp.bfloat16)
            ref, at = spans[k]
            values = jnp.concatenate([ref[at, 256 + h * 128 : 384 + h * 128, :], ones], axis=0)
            acc = acc + jnp.dot(values, p, preferred_element_type=jnp.float32)
        m_ref[...] = jnp.broadcast_to(new, m_ref.shape)
        acc_ref[...] = acc

    if last:
        for r in range(4):
            for h in range(2):
                at = slice((2 * r + h) * 128, (2 * r + h + 1) * 128)
                v = acc_ref[0:128, at] / acc_ref[128:129, at]
                out[r, :, h * 128 : (h + 1) * 128] = v.T.astype(jnp.bfloat16)


def attend(top, q, query_place, limit, state, blocks, last):
    first = state is None
    state_in = [] if first else list(state)
    spans = sum(b.shape[0] for b in blocks)
    state_shapes = (
        jax.ShapeDtypeStruct((8, 1024), jnp.float32),
        jax.ShapeDtypeStruct((144, 1024), jnp.float32),
    )
    if last:
        out_shape = jax.ShapeDtypeStruct((4, ROWS, 256), jnp.bfloat16)
        out_specs = vmem_specs(1)[0]
        scratch = [pltpu.VMEM(s.shape, s.dtype) for s in state_shapes]
    else:
        out_shape = state_shapes
        out_specs = tuple(vmem_specs(2))
        scratch = []
    return pl.pallas_call(
        functools.partial(attend_kernel, len(blocks), first, last),
        out_shape=out_shape,
        in_specs=[SMEM_SPEC] + vmem_specs(3 + len(state_in) + len(blocks)),
        out_specs=out_specs,
        scratch_shapes=scratch,
        compiler_params=pltpu.CompilerParams(vmem_limit_bytes=24 * 2**20),
        cost_estimate=pl.CostEstimate(
            flops=spans * 12 * 10**8, bytes_accessed=2**21, transcendentals=spans * 2**19
        ),
    )(top, q, query_place, limit, *state_in, *blocks)


def on_device(
    hidden,
    norm_gain,
    w_query,
    key_weight_matrix,
    value_weight_matrix,
    key_cache,
    stored_value_cache,
    sel_rows,
    span_place,
):
    c = lax.axis_index("ctx")
    t = lax.axis_index("tp")
    z = c // GROUP
    g = c % GROUP
    core = g % 2
    xlo = g // 2
    xhi = t // 4
    y = t % 4

    info = jnp.concatenate([sel_rows, jnp.broadcast_to(span_place[:, None], (1, ROWS))], axis=0)
    info_x = to_group(info, 2)
    info_c = to_group(jnp.stack([info, info_x]), 1)
    info = jnp.stack([info, info_c[0], info_x, info_c[1]])
    sel_rel = info[:, 0, :]
    place_rel = info[:, 1, 0]

    def by_core(mine, theirs, axis):
        return jnp.where(core == 0, jnp.stack([mine, theirs], axis), jnp.stack([theirs, mine], axis))

    def by_xlo(mine, theirs, axis):
        return jnp.where(xlo == 0, jnp.stack([mine, theirs], axis), jnp.stack([theirs, mine], axis))

    def half(w, h):
        return jnp.concatenate([w[:, 32 * h : 32 * h + 32], w[:, 64 + 32 * h : 96 + 32 * h]], axis=1)

    def pack(w):
        return w.reshape(4, 64, 64).transpose(1, 0, 2).reshape(64, 256)

    pieces = jnp.stack(
        [
            jnp.concatenate(
                [
                    w_query[:, 256 * j : 256 * (j + 1)],
                    pack(half(value_weight_matrix if j % 2 else key_weight_matrix, j // 2)),
                ],
                axis=0,
            )
            for j in range(4)
        ]
    )
    hold = lax.optimization_barrier
    hidden_x = to_group(hidden[0], 2)
    shards = [lax.dynamic_index_in_dim(pieces, g, 0, keepdims=True)]
    for d in (1, 2, 3):
        shards.append(to_group(lax.dynamic_index_in_dim(pieces, g ^ d, 0, keepdims=True), d))
    block = xor_order(jnp.concatenate(shards, axis=0), core, xlo)
    pair = by_xlo(hidden[0], hidden_x, 0)
    rows = by_core(pair, to_group(pair, 1), 1).reshape(4, ROWS, CHUNK)

    block, pair = hold((block, pair))
    r1, l1 = shift_z(block, 1), shift_z(block, -1)
    far = along_xh(pair)
    y1 = along_y(rows)
    r1, l1, far, y1 = hold((r1, l1, far, y1))
    r2, l2 = shift_z(r1, 1), shift_z(l1, -1)
    far = by_core(far, to_group(far, 1), 1).reshape(4, ROWS, CHUNK)
    f1 = along_y(far)
    y1_other = to_group(y1, 1)
    caches = jnp.stack([key_cache[0], stored_value_cache[0]])
    caches_x = to_group(caches, 2)
    r2, l2, f1, caches_x = hold((r2, l2, f1, caches_x))
    r3, l3 = shift_z(r2, 1), shift_z(l2, -1)
    y2 = along_y(jnp.where(core == 0, y1, f1))
    f1_other = to_group(f1, 1)
    caches_c, caches_d = to_group(caches, 1), to_group(caches_x, 1)
    r3, l3, y2, caches_c, caches_d = hold((r3, l3, y2, caches_c, caches_d))
    r4k = shift_z(r3[:, 256:], 1)
    r4, l4 = shift_z(r3[:2, :256], 1), shift_z(l3[2:, :256], -1)
    y2_other = to_group(y2, 1)
    arrays = [rows, far, y1, y1_other, f1, f1_other, y2, y2_other]
    down = (y + 3 + 2 * core) % 4
    up = (y + 1 + 2 * core) % 4
    across = (y + 2) % 4
    row_ids = [
        t,
        t ^ 4,
        xhi * 4 + down,
        xhi * 4 + up,
        (1 - xhi) * 4 + down,
        (1 - xhi) * 4 + up,
        (xhi ^ core) * 4 + across,
        (xhi ^ (1 - core)) * 4 + across,
    ]
    row_ids = jnp.stack(row_ids + [j ^ g for j in range(4)]).astype(jnp.int32)
    weight_ids = jnp.stack([(z + s) % 8 for s in (0, 7, 1, 6, 2, 5, 3, 4)]).astype(jnp.int32)

    positions = (place_rel[:, None] * SPAN + sel_rel).reshape(GROUP * ROWS)
    half_size = HEAD_WIDTH // 2
    freqs = 500000.0 ** (-2.0 * jnp.arange(half_size, dtype=jnp.float32) / HEAD_WIDTH)
    angles = positions.astype(jnp.float32)[:, None] * freqs[None, :]
    cos, sin = jnp.cos(angles), jnp.sin(angles)
    cos_half = jnp.where(xlo == 0, cos[:, :32], cos[:, 32:])
    sin_half = jnp.where(xlo == 0, sin[:, :32], sin[:, 32:])
    cos_half = jnp.where(core == 0, cos_half, 1.0)
    sin_half = jnp.where(core == 0, sin_half, 0.0)
    tables = (
        jnp.concatenate([cos, cos], axis=1),
        jnp.concatenate([-sin, sin], axis=1),
        jnp.concatenate([cos_half] * 4, axis=1),
        jnp.concatenate([-sin_half, sin_half] * 2, axis=1),
    )
    gain = norm_gain.astype(jnp.float32).reshape(8, 1, CHUNK)

    normed = normalize(row_ids, gain, arrays)
    cos_q, sin_q, cos_kv, sin_kv = tables
    weights = [block, r1, l1, r2, l2, r3, l3]
    kv_piece = project(project_kv_kernel, (2, ROWS, 128), weight_ids, normed, cos_kv, sin_kv, weights + [r4k])
    q = project(project_q_kernel, (128, 1024), weight_ids, normed, cos_q, sin_q, weights + [r4, l4])

    got = [kv_piece] + [to_group(kv_piece, d) for d in (1, 2, 3)]
    blend_info = jnp.concatenate([jnp.stack([core, xlo]).astype(jnp.int32), place_rel])
    mixed_key_cache, mixed_value_cache, mine, theirs = blend(
        blend_info, sel_rel, got, [caches, caches_c, caches_x, caches_d]
    )

    limit = jnp.broadcast_to(jnp.concatenate([sel_rel, sel_rel], axis=1).reshape(1, 1024), (8, 1024))
    query_place = jnp.broadcast_to(jnp.repeat(place_rel.astype(jnp.float32), 256)[None], (8, 1024))
    top = jnp.max(place_rel)[None]
    right, left = shift_z(mine, 1), shift_z(mine, -1)
    state = attend(top, q, query_place, limit, None, [mine, theirs], False)
    for n in (1, 2, 3, 4):
        right, left, state = hold((right, left, state))
        if n < 3:
            ahead = shift_z(right, 1), shift_z(left, -1)
        elif n == 3:
            ahead = shift_z(right[:1], 1), shift_z(left[1:], -1)
        swapped = [to_group(right, 1), to_group(left, 1)]
        state = attend(top, q, query_place, limit, state, [right, left], False)
        state = attend(top, q, query_place, limit, state, swapped, n == 4)
        right, left = ahead

    out = [state[0]] + [to_group(state[d], d) for d in (1, 2, 3)]
    attended = xor_order(jnp.concatenate(out, axis=1), core, xlo, axis=1)
    return (attended[None], mixed_key_cache[None], mixed_value_cache[None])


def solution(mesh):
    return jax.shard_map(
        on_device,
        mesh=mesh,
        in_specs=(
            P("ctx", None, "tp"),
            P(),
            P("ctx", "tp"),
            P("ctx", "tp"),
            P("ctx", "tp"),
            P("ctx", None, "tp"),
            P("ctx", None, "tp"),
            P("ctx", None),
            P("ctx"),
        ),
        out_specs=(P("ctx", None, "tp"), P("ctx", None, "tp"), P("ctx", None, "tp")),
        check_vma=False,
    )
```

```python
import functools
import math

import jax
import jax.numpy as jnp
from jax import lax
from jax.experimental import pallas as pl
from jax.experimental.pallas import tpu as pltpu
from jax.sharding import PartitionSpec as P

HEAD_WIDTH = 128
ROWS = 128
SPAN = 512
WIDTH = 8192
Z = 8
GROUP = 4
CTX = 32
TP = 8
CHUNK = 1024
NEGATIVE = -1e30
BLOCK_ROWS = 528
SCALE2 = HEAD_WIDTH ** (-0.5) * math.log2(math.e)


def to_group(x, d):
    return lax.ppermute(x, "ctx", [(c, (c // GROUP) * GROUP + ((c % GROUP) ^ d)) for c in range(CTX)])


def shift_z(x, s):
    return lax.ppermute(x, "ctx", [(c, (c + GROUP * s) % CTX) for c in range(CTX)])


def along_y(x):
    def place(c, t, s):
        return c * TP + (t // 4) * 4 + (t + s) % 4

    return lax.ppermute(
        x,
        ("ctx", "tp"),
        [(place(c, t, 0), place(c, t, 1 if c % 2 == 0 else -1)) for c in range(CTX) for t in range(TP)],
    )


def along_xh(x):
    return lax.ppermute(x, "tp", [(t, t ^ 4) for t in range(TP)])


def xor_order(x, core, xlo, axis=0):
    a, b, c, d = jnp.split(x, 4, axis=axis)
    swapped = jnp.concatenate([b, a, d, c], axis=axis)
    x = jnp.where(core == 1, swapped, x)
    a, b, c, d = jnp.split(x, 4, axis=axis)
    swapped = jnp.concatenate([c, d, a, b], axis=axis)
    return jnp.where(xlo == 1, swapped, x)


def vmem_specs(n):
    return [pl.BlockSpec(memory_space=pltpu.VMEM)] * n


SMEM_SPEC = pl.BlockSpec(memory_space=pltpu.SMEM)


def squares_kernel(*refs):
    arrays, out = refs[:-1], refs[-1]

    def rows_step(k, carry):
        rows = pl.ds(pl.multiple_of(k * 16, 16), 16)
        for j in range(4):
            total = jnp.zeros((16, 128), jnp.float32)
            for ref in arrays:
                v = ref[j, rows, :].astype(jnp.float32)
                v = v * v
                for lane in range(0, CHUNK, 128):
                    total = total + v[:, lane : lane + 128]
            out[j, rows, :] = total
        return carry

    lax.fori_loop(0, ROWS // 16, rows_step, 0)


def squares(arrays):
    return pl.pallas_call(
        squares_kernel,
        out_shape=jax.ShapeDtypeStruct((4, ROWS, 128), jnp.float32),
        in_specs=vmem_specs(len(arrays)),
        out_specs=vmem_specs(1)[0],
        compiler_params=pltpu.CompilerParams(vmem_limit_bytes=16 * 2**20),
        cost_estimate=pl.CostEstimate(flops=2 * 10**9, bytes_accessed=5 * 2**20, transcendentals=0),
    )(*arrays)


def normalize_kernel(*refs):
    ids, gain, partial = refs[:3]
    arrays = refs[3:11]
    normed = refs[11]

    def rows_step(k, carry):
        rows = pl.ds(pl.multiple_of(k * 16, 16), 16)
        for j in range(4):
            to = ids[8 + j] * ROWS + k * 16
            total = partial[j, rows, :]
            for ref in arrays[5:]:
                v = ref[j, rows, :].astype(jnp.float32)
                v = v * v
                for lane in range(0, CHUNK, 128):
                    total = total + v[:, lane : lane + 128]
            inv = lax.rsqrt(jnp.sum(total, axis=1, keepdims=True) / WIDTH + 1e-05)
            for i, ref in enumerate(arrays):
                place = ids[i]
                v = ref[j, rows, :].astype(jnp.float32)
                v = (v * inv * gain[place]).astype(jnp.bfloat16)
                normed[place, pl.ds(pl.multiple_of(to, 16), 16), :] = v
        return carry

    lax.fori_loop(0, ROWS // 16, rows_step, 0)


def normalize(ids, gain, partial, arrays):
    return pl.pallas_call(
        normalize_kernel,
        out_shape=jax.ShapeDtypeStruct((8, 512, CHUNK), jnp.bfloat16),
        in_specs=[SMEM_SPEC] + vmem_specs(10),
        out_specs=vmem_specs(1)[0],
        compiler_params=pltpu.CompilerParams(vmem_limit_bytes=24 * 2**20),
        cost_estimate=pl.CostEstimate(flops=6 * 10**9, bytes_accessed=16 * 2**20, transcendentals=0),
    )(ids, gain, partial, *arrays)


def multiply_add(acc, ids, normed, weights, part):
    for s, ref in enumerate(weights):
        shards = ref.shape[0]
        first = 512 if s == 8 else 0
        x = normed[ids[min(s, 7)], :, first : first + shards * 256]
        w = jnp.concatenate([part(ref, j) for j in range(shards)], axis=0)
        v = jnp.dot(x, w, preferred_element_type=jnp.float32)
        if s == 0:
            acc[...] = v
        else:
            acc[...] += v


def project_kv_kernel(ids, normed, cos_kv, sin_kv, *refs):
    weights, (kv_out, acc) = refs[:-2], refs[-2:]
    row_block = lax.broadcasted_iota(jnp.int32, (256, 256), 0) // 64
    col_block = lax.broadcasted_iota(jnp.int32, (256, 256), 1) // 64
    same = row_block == col_block

    def spread(ref, j):
        tiled = jnp.concatenate([ref[j, ref.shape[1] - 64 :, :]] * 4, axis=0)
        return jnp.where(same, tiled, jnp.zeros_like(tiled))

    multiply_add(acc, ids, normed, weights, spread)
    lane = lax.broadcasted_iota(jnp.int32, (ROWS, 128), 1)
    pieces = []
    for r in range(4):
        rows = slice(r * ROWS, (r + 1) * ROWS)
        v = acc[rows, :128] + acc[rows, 128:]
        v = v + pltpu.roll(v, 64, axis=1)
        pieces.append(v * cos_kv[rows, :] + pltpu.roll(v, 32, axis=1) * sin_kv[rows, :])
    for r in range(2):
        kv_out[r] = jnp.where(lane < 64, pieces[r], pieces[r + 2]).astype(jnp.bfloat16)


def project_q_kernel(ids, normed, cos_q, sin_q, *refs):
    weights, (q_out, acc) = refs[:-2], refs[-2:]
    multiply_add(acc, ids, normed, weights, lambda ref, j: ref[j, :256, :])
    for r in range(4):
        rows = slice(r * ROWS, (r + 1) * ROWS)
        for h in range(2):
            v = acc[rows, h * 128 : (h + 1) * 128]
            v = v * cos_q[rows, :] + pltpu.roll(v, 64, axis=1) * sin_q[rows, :]
            q_out[:, (2 * r + h) * 128 : (2 * r + h + 1) * 128] = v.T.astype(jnp.bfloat16)


def project(kernel, shape, ids, normed, cos, sin, weights):
    return pl.pallas_call(
        kernel,
        out_shape=jax.ShapeDtypeStruct(shape, jnp.bfloat16),
        in_specs=[SMEM_SPEC] + vmem_specs(3 + len(weights)),
        out_specs=vmem_specs(1)[0],
        scratch_shapes=[pltpu.VMEM((512, 256), jnp.float32)],
        compiler_params=pltpu.CompilerParams(vmem_limit_bytes=24 * 2**20),
        cost_estimate=pl.CostEstimate(flops=4 * 10**9, bytes_accessed=12 * 2**20, transcendentals=0),
    )(ids, normed, cos, sin, *weights)


def blend_kernel(info, sel, g0, g1, g2, g3, c0, c1, c2, c3, key_out, value_out, own_block, other_block):
    core, xlo = info[0], info[1]
    lane = lax.broadcasted_iota(jnp.int32, (ROWS, 128), 1)
    row = lax.broadcasted_iota(jnp.int32, (SPAN, ROWS), 0)
    pieces = []
    for ref in (g0, g1, g2, g3):
        ends = []
        for r in range(2):
            v = ref[r].astype(jnp.float32)
            turned = pltpu.roll(v, 64, axis=1)
            ends.append((jnp.where(lane < 64, v, turned), jnp.where(lane < 64, turned, v)))
        pieces.append([ends[0][0], ends[1][0], ends[0][1], ends[1][1]])

    def join(a, b):
        low = jnp.where(xlo == 0, a, b)
        high = jnp.where(xlo == 0, b, a)
        new = jnp.where(lane < 96, pltpu.roll(low, 32, axis=1), high)
        new = jnp.where(lane < 64, pltpu.roll(high, 32, axis=1), new)
        return jnp.where(lane < 32, low, new).astype(jnp.bfloat16)

    for d, caches in enumerate((c0, c1, c2, c3)):
        block, j = (other_block if d % 2 else own_block), d // 2
        got = [pieces[e][d ^ e] for e in range(4)]
        new_key = join(jnp.where(core == 0, got[0], got[1]), jnp.where(core == 0, got[2], got[3]))
        new_value = join(jnp.where(core == 0, got[1], got[0]), jnp.where(core == 0, got[3], got[2]))
        hit = (row == sel[d : d + 1, :]).astype(jnp.float32)
        chosen = jnp.sum(hit, axis=1, keepdims=True) > 0.0
        hit = hit.astype(jnp.bfloat16)
        mixed = []
        for k, new in enumerate((new_key, new_value)):
            placed = jnp.dot(hit, new, preferred_element_type=jnp.float32)
            mixed.append(jnp.where(chosen, placed, caches[k].astype(jnp.float32)))
        if d == 0:
            key_out[...] = mixed[0].astype(jnp.bfloat16)
            value_out[...] = mixed[1].astype(jnp.bfloat16)
        block[j, 0:256, 0:128] = mixed[0][:256].astype(jnp.bfloat16)
        block[j, 0:256, 128:256] = mixed[0][256:].astype(jnp.bfloat16)
        for h in range(2):
            block[j, 256 + 128 * h : 384 + 128 * h, :] = mixed[1][256 * h : 256 * (h + 1)].T.astype(jnp.bfloat16)
        place = info[2 + d].astype(jnp.float32)
        block[j, 512:528, :] = jnp.full((16, 256), place, jnp.float32).astype(jnp.bfloat16)


def blend(info, sel, got, caches):
    cache = jax.ShapeDtypeStruct((SPAN, HEAD_WIDTH), jnp.bfloat16)
    return pl.pallas_call(
        blend_kernel,
        out_shape=(cache, cache) + (jax.ShapeDtypeStruct((2, BLOCK_ROWS, 256), jnp.bfloat16),) * 2,
        in_specs=[SMEM_SPEC] + vmem_specs(9),
        out_specs=tuple(vmem_specs(4)),
        compiler_params=pltpu.CompilerParams(vmem_limit_bytes=16 * 2**20),
        cost_estimate=pl.CostEstimate(flops=4 * 10**9, bytes_accessed=2**22, transcendentals=0),
    )(info, sel, *got, *caches)


def attend_kernel(count, first, last, top, q, query_place, limit, *refs):
    if not first:
        m_in, acc_in = refs[:2]
        refs = refs[2:]
    blocks, refs = refs[:count], refs[count:]
    if last:
        out, m_ref, acc_ref = refs
    else:
        m_ref, acc_ref = refs
    spans = [(ref, k) for ref in blocks for k in range(ref.shape[0])]
    ones = jnp.ones((16, 256), jnp.bfloat16)
    if first:
        m_ref[...] = jnp.full_like(m_ref, NEGATIVE)
        acc_ref[...] = jnp.zeros_like(acc_ref)
    else:
        m_ref[...] = m_in[...]
        acc_ref[...] = acc_in[...]
    places = [jnp.max(ref[k, 512:528, 0:128].astype(jnp.float32)) for ref, k in spans]
    least = functools.reduce(jnp.minimum, places)

    @pl.when(least <= top[0].astype(jnp.float32))
    def _():
        mine = query_place[0:1, :]
        allowed = [(p <= mine) if first else (p < mine) for p in places]
        chunks = []
        for k, (ref, at) in enumerate(spans):
            for h in range(2):
                s = jnp.dot(ref[at, 0:256, h * 128 : (h + 1) * 128], q[...], preferred_element_type=jnp.float32)
                if first:
                    row = lax.broadcasted_iota(jnp.int32, s.shape, 0) + h * 256
                    s = jnp.where(row <= jnp.where(places[k] == mine, limit[0:1, :], SPAN), s, NEGATIVE)
                chunks.append((s, k, h))
        old = m_ref[0:1, :]
        new = old
        for s, k, h in chunks:
            new = jnp.maximum(new, jnp.where(allowed[k], jnp.max(s, axis=0, keepdims=True), NEGATIVE))
        acc = acc_ref[...] * jnp.exp2((old - new) * SCALE2)
        against = [jnp.where(a, new, -NEGATIVE) for a in allowed]
        for s, k, h in chunks:
            p = jnp.exp2((s - against[k]) * SCALE2).astype(jnp.bfloat16)
            ref, at = spans[k]
            values = jnp.concatenate([ref[at, 256 + h * 128 : 384 + h * 128, :], ones], axis=0)
            acc = acc + jnp.dot(values, p, preferred_element_type=jnp.float32)
        m_ref[...] = jnp.broadcast_to(new, m_ref.shape)
        acc_ref[...] = acc

    if last:
        for r in range(4):
            for h in range(2):
                at = slice((2 * r + h) * 128, (2 * r + h + 1) * 128)
                v = acc_ref[0:128, at] / acc_ref[128:129, at]
                out[r, :, h * 128 : (h + 1) * 128] = v.T.astype(jnp.bfloat16)


def attend(top, q, query_place, limit, state, blocks, last):
    first = state is None
    state_in = [] if first else list(state)
    spans = sum(b.shape[0] for b in blocks)
    state_shapes = (
        jax.ShapeDtypeStruct((8, 1024), jnp.float32),
        jax.ShapeDtypeStruct((144, 1024), jnp.float32),
    )
    if last:
        out_shape = jax.ShapeDtypeStruct((4, ROWS, 256), jnp.bfloat16)
        out_specs = vmem_specs(1)[0]
        scratch = [pltpu.VMEM(s.shape, s.dtype) for s in state_shapes]
    else:
        out_shape = state_shapes
        out_specs = tuple(vmem_specs(2))
        scratch = []
    return pl.pallas_call(
        functools.partial(attend_kernel, len(blocks), first, last),
        out_shape=out_shape,
        in_specs=[SMEM_SPEC] + vmem_specs(3 + len(state_in) + len(blocks)),
        out_specs=out_specs,
        scratch_shapes=scratch,
        compiler_params=pltpu.CompilerParams(vmem_limit_bytes=24 * 2**20),
        cost_estimate=pl.CostEstimate(
            flops=spans * 12 * 10**8, bytes_accessed=2**21, transcendentals=spans * 2**19
        ),
    )(top, q, query_place, limit, *state_in, *blocks)


def on_device(
    hidden,
    norm_gain,
    w_query,
    key_weight_matrix,
    value_weight_matrix,
    key_cache,
    stored_value_cache,
    sel_rows,
    span_place,
):
    c = lax.axis_index("ctx")
    t = lax.axis_index("tp")
    z = c // GROUP
    g = c % GROUP
    core = g % 2
    xlo = g // 2
    xhi = t // 4
    y = t % 4

    info = jnp.concatenate([sel_rows, jnp.broadcast_to(span_place[:, None], (1, ROWS))], axis=0)
    info_x = to_group(info, 2)
    info_c = to_group(jnp.stack([info, info_x]), 1)
    info = jnp.stack([info, info_c[0], info_x, info_c[1]])
    sel_rel = info[:, 0, :]
    place_rel = info[:, 1, 0]

    def by_core(mine, theirs, axis):
        return jnp.where(core == 0, jnp.stack([mine, theirs], axis), jnp.stack([theirs, mine], axis))

    def by_xlo(mine, theirs, axis):
        return jnp.where(xlo == 0, jnp.stack([mine, theirs], axis), jnp.stack([theirs, mine], axis))

    def half(w, h):
        return jnp.concatenate([w[:, 32 * h : 32 * h + 32], w[:, 64 + 32 * h : 96 + 32 * h]], axis=1)

    def pack(w):
        return w.reshape(4, 64, 64).transpose(1, 0, 2).reshape(64, 256)

    pieces = jnp.stack(
        [
            jnp.concatenate(
                [
                    w_query[:, 256 * j : 256 * (j + 1)],
                    pack(half(value_weight_matrix if j % 2 else key_weight_matrix, j // 2)),
                ],
                axis=0,
            )
            for j in range(4)
        ]
    )
    hold = lax.optimization_barrier
    hidden_x = to_group(hidden[0], 2)
    shards = [lax.dynamic_index_in_dim(pieces, g, 0, keepdims=True)]
    for d in (1, 2, 3):
        shards.append(to_group(lax.dynamic_index_in_dim(pieces, g ^ d, 0, keepdims=True), d))
    block = xor_order(jnp.concatenate(shards, axis=0), core, xlo)
    pair = by_xlo(hidden[0], hidden_x, 0)
    rows = by_core(pair, to_group(pair, 1), 1).reshape(4, ROWS, CHUNK)

    block, pair = hold((block, pair))
    r1, l1 = shift_z(block, 1), shift_z(block, -1)
    far = along_xh(pair)
    y1 = along_y(rows)
    r1, l1, far, y1 = hold((r1, l1, far, y1))
    r2, l2 = shift_z(r1, 1), shift_z(l1, -1)
    far = by_core(far, to_group(far, 1), 1).reshape(4, ROWS, CHUNK)
    f1 = along_y(far)
    y1_other = to_group(y1, 1)
    caches = jnp.stack([key_cache[0], stored_value_cache[0]])
    caches_x = to_group(caches, 2)
    k0, kr1, kl1 = block[:, 256:], r1[:, 256:], l1[:, 256:]
    r2, l2, f1, caches_x, k0, kr1, kl1 = hold((r2, l2, f1, caches_x, k0, kr1, kl1))
    r3, l3 = shift_z(r2, 1), shift_z(l2, -1)
    y2 = along_y(jnp.where(core == 0, y1, f1))
    f1_other = to_group(f1, 1)
    caches_c, caches_d = to_group(caches, 1), to_group(caches_x, 1)
    kr2, kl2 = r2[:, 256:], l2[:, 256:]
    partial = squares([rows, far, y1, y1_other, f1])
    r3, l3, y2, caches_c, caches_d, kr2, kl2, partial = hold(
        (r3, l3, y2, caches_c, caches_d, kr2, kl2, partial)
    )
    r4k = shift_z(r3[:, 256:], 1)
    r4, l4 = shift_z(r3[:2, :256], 1), shift_z(l3[2:, :256], -1)
    y2_other = to_group(y2, 1)
    arrays = [rows, far, y1, y1_other, f1, f1_other, y2, y2_other]
    down = (y + 3 + 2 * core) % 4
    up = (y + 1 + 2 * core) % 4
    across = (y + 2) % 4
    row_ids = [
        t,
        t ^ 4,
        xhi * 4 + down,
        xhi * 4 + up,
        (1 - xhi) * 4 + down,
        (1 - xhi) * 4 + up,
        (xhi ^ core) * 4 + across,
        (xhi ^ (1 - core)) * 4 + across,
    ]
    row_ids = jnp.stack(row_ids + [j ^ g for j in range(4)]).astype(jnp.int32)
    weight_ids = jnp.stack([(z + s) % 8 for s in (0, 7, 1, 6, 2, 5, 3, 4)]).astype(jnp.int32)

    positions = (place_rel[:, None] * SPAN + sel_rel).reshape(GROUP * ROWS)
    half_size = HEAD_WIDTH // 2
    freqs = 500000.0 ** (-2.0 * jnp.arange(half_size, dtype=jnp.float32) / HEAD_WIDTH)
    angles = positions.astype(jnp.float32)[:, None] * freqs[None, :]
    cos, sin = jnp.cos(angles), jnp.sin(angles)
    cos_half = jnp.where(xlo == 0, cos[:, :32], cos[:, 32:])
    sin_half = jnp.where(xlo == 0, sin[:, :32], sin[:, 32:])
    cos_half = jnp.where(core == 0, cos_half, 1.0)
    sin_half = jnp.where(core == 0, sin_half, 0.0)
    tables = (
        jnp.concatenate([cos, cos], axis=1),
        jnp.concatenate([-sin, sin], axis=1),
        jnp.concatenate([cos_half] * 4, axis=1),
        jnp.concatenate([-sin_half, sin_half] * 2, axis=1),
    )
    gain = norm_gain.astype(jnp.float32).reshape(8, 1, CHUNK)

    normed = normalize(row_ids, gain, partial, arrays)
    cos_q, sin_q, cos_kv, sin_kv = tables
    weights = [block, r1, l1, r2, l2, r3, l3]
    kv_piece = project(project_kv_kernel, (2, ROWS, 128), weight_ids, normed, cos_kv, sin_kv, [k0, kr1, kl1, kr2, kl2, r3, l3, r4k])
    q = project(project_q_kernel, (128, 1024), weight_ids, normed, cos_q, sin_q, weights + [r4, l4])

    got = [kv_piece] + [to_group(kv_piece, d) for d in (1, 2, 3)]
    blend_info = jnp.concatenate([jnp.stack([core, xlo]).astype(jnp.int32), place_rel])
    mixed_key_cache, mixed_value_cache, mine, theirs = blend(
        blend_info, sel_rel, got, [caches, caches_c, caches_x, caches_d]
    )

    limit = jnp.broadcast_to(jnp.concatenate([sel_rel, sel_rel], axis=1).reshape(1, 1024), (8, 1024))
    query_place = jnp.broadcast_to(jnp.repeat(place_rel.astype(jnp.float32), 256)[None], (8, 1024))
    top = jnp.max(place_rel)[None]
    right, left = shift_z(mine, 1), shift_z(mine, -1)
    state = attend(top, q, query_place, limit, None, [mine, theirs], False)
    for n in (1, 2, 3, 4):
        right, left, state = hold((right, left, state))
        if n < 3:
            ahead = shift_z(right, 1), shift_z(left, -1)
        elif n == 3:
            ahead = shift_z(right[:1], 1), shift_z(left[1:], -1)
        swapped = [to_group(right, 1), to_group(left, 1)]
        state = attend(top, q, query_place, limit, state, [right, left], False)
        state = attend(top, q, query_place, limit, state, swapped, n == 4)
        right, left = ahead

    out = [state[0]] + [to_group(state[d], d) for d in (1, 2, 3)]
    attended = xor_order(jnp.concatenate(out, axis=1), core, xlo, axis=1)
    return (attended[None], mixed_key_cache[None], mixed_value_cache[None])


def solution(mesh):
    return jax.shard_map(
        on_device,
        mesh=mesh,
        in_specs=(
            P("ctx", None, "tp"),
            P(),
            P("ctx", "tp"),
            P("ctx", "tp"),
            P("ctx", "tp"),
            P("ctx", None, "tp"),
            P("ctx", None, "tp"),
            P("ctx", None),
            P("ctx"),
        ),
        out_specs=(P("ctx", None, "tp"), P("ctx", None, "tp"), P("ctx", None, "tp")),
        check_vma=False,
    )
```
